32 devices in a mesh: exp: 8 (over y, x, core), rep: 4 (over z).
Axes of the slice: x: 2, y: 2, z: 4, core: 2. Of those that a mesh axis runs over, the one named last changes fastest.
Arguments:
- tokens: bfloat16 [256, 6144], P(('exp', 'rep')), may hold values from -6 to 6
- slot_index: int32 [256], P(('exp', 'rep')), may hold values from 0 to 2, as said below
- saved_inputs: bfloat16 [4, 512, 6144], P('rep'), may hold values from -6 to 6
- cotangents: bfloat16 [4, 512, 2, 8192], P('rep', None, None, 'exp'), may hold values from -0.046875 to 0.046875
- master: float32 [6144, 2, 8192], P('rep', None, 'exp'), may hold values from -0.078125 to 0.078125
- moment1: float32 [6144, 2, 8192], P('rep', None, 'exp'), may hold values from -0.046875 to 0.046875
- moment2: float32 [6144, 2, 8192], P('rep', None, 'exp'), may hold values from 3e-07 to 3e-05
Outputs:
- new_master: float32 [6144, 2, 8192], P('rep', None, 'exp')
- new_moment1: float32 [6144, 2, 8192], P('rep', None, 'exp')
- new_moment2: float32 [6144, 2, 8192], P('rep', None, 'exp')
- hidden: bfloat16 [4, 16, 8192], P('rep', None, 'exp')
The draws below stay inside these ranges and needn't reach their ends.
Inputs may be any that keep to these rules, and one draw needn't show every extreme that they name: `slot_index`: in each aligned block of 8 tokens every slot 0 to 1 is held by exactly one token; the other tokens carry 2, meaning not routed to this expert.
All inputs are finite; a program needn't handle non-finite values.
Results may differ from the reference program's by a relative error of at most 0.0075.
Values may be sent and summed in bfloat16 or wider, within the bound.
A program may use at most 192 MiB of HBM per device.

```python
import math
import jax
import jax.numpy as jnp
from jax import lax

D = 6144
FF = 8192
SAVED = 512
TOK_DEV = 8
STEP = 100
CAP = 2
TOKENS = 256
N_EXP = 8
N_REP = 4


def draw_slot_index(key, part):
    block_count = TOKENS // TOK_DEV
    block_keys = jax.random.split(key, block_count)
    orders = jax.vmap(lambda one_key: jax.random.permutation(one_key, TOK_DEV))(block_keys)
    return jnp.minimum(orders, CAP).astype(jnp.int32).reshape(TOKENS)


def raised(result, own_key, source, target, parts, factor):
    owner, partner = [(jnp.arange(result.shape[dim]) // (result.shape[dim] // parts)).reshape([-1 if axis == dim else 1 for axis in range(result.ndim)]) for dim in (source, target)]
    chosen = jax.random.permutation(own_key, parts)[partner]
    strong = (owner == chosen) | (owner == (partner + parts // 2) % parts)
    return jnp.where(strong, factor * result, result)


def block_scale(key, shape, cuts, smallest, high):
    loudness, own = 1.0, jax.random.fold_in(key, 6)
    for position, shards_of in cuts:
        draws = jnp.exp(jax.random.uniform(jax.random.fold_in(own, position), (shards_of,), jnp.float32, smallest / len(cuts), high / len(cuts)))
        loudness = loudness * jnp.repeat(draws, shape[position] // shards_of).reshape([-1 if axis == position else 1 for axis in range(len(shape))])
    return loudness


def noise(key, dims, width, most, cuts=(), held_as=jnp.bfloat16):
    result = width * jax.random.normal(key, dims, jnp.float32)
    if cuts:
        result = result * block_scale(key, dims, cuts, -0.22, 0.18)
    return jnp.clip(result, -most, most).astype(held_as)


def heavy_noise(own_key, extent, deviation, bound, pieces, heavy, kind=jnp.bfloat16):
    entries = deviation * jax.random.normal(own_key, extent, jnp.float32)
    if pieces:
        entries = entries * block_scale(own_key, extent, pieces, -0.22, 0.18)
    return jnp.clip(raised(entries, jax.random.fold_in(own_key, 3), *heavy), -bound, bound).astype(kind)


def setup_inputs(seed: int = 0) -> dict:
    key_of = jax.random.split(jax.random.key(seed), 8)
    tokens = noise(key_of[0], (TOKENS, D), 1.0, 6.0, ((0, 32),))
    slot_index = draw_slot_index(jax.random.fold_in(key_of[7], 71), 0)
    saved_inputs = heavy_noise(key_of[2], (N_REP, SAVED, D), 1.0, 6.0, ((0, 4),), (0, 2, 4, 2.0))
    cotangents = noise(key_of[3], (N_REP, SAVED, 2, FF), 0.003, 0.046875, ((0, 4), (3, 8)))
    master = noise(key_of[4], (D, 2, FF), D ** -0.5, 0.078125, ((0, 4), (2, 8)), jnp.float32)
    moment1 = noise(key_of[5], (D, 2, FF), 0.003, 0.046875, ((0, 4), (2, 8)), jnp.float32)
    moment2 = jnp.clip(jnp.exp(math.log(2.9999999242136255e-05) - 4.6051701 * jax.random.uniform(key_of[6], (D, 2, FF), jnp.float32) ** block_scale(key_of[6], (D, 2, FF), ((0, 4), (2, 8)), -0.2, 0.2)), 3.000000106112566e-07, 2.9999999242136255e-05)
    return {"tokens": tokens, "slot_index": slot_index, "saved_inputs": saved_inputs, "cotangents": cotangents, "master": master, "moment1": moment1, "moment2": moment2}


def reference(tokens, slot_index, saved_inputs, cotangents, master, moment1, moment2):

    def add_replica(total, items):
        rows_in, cotangent = items
        part = jnp.dot(rows_in.T, cotangent.reshape(SAVED, 2 * FF), preferred_element_type=jnp.float32)
        rounded = lax.optimization_barrier(part.astype(jnp.bfloat16))
        return (total + rounded.astype(jnp.float32), None)
    total, _ = lax.scan(add_replica, jnp.zeros((D, 2 * FF), jnp.float32), (saved_inputs, cotangents))
    average = (total / N_REP).reshape(D, 2, FF)
    new_first = 0.9 * moment1 + 0.1 * average
    new_second = 0.999 * moment2 + 0.001 * average * average
    correct_one = 1.0 - 0.9 ** STEP
    correct_two = 1.0 - 0.999 ** STEP
    ratio = new_first / correct_one / (jnp.sqrt(new_second / correct_two) + 1e-08)
    new_master = master - 0.001 * (ratio + 0.1 * master)
    weights = new_master.astype(jnp.bfloat16)
    blocks = tokens.reshape(N_EXP, N_REP, TOK_DEV, D).astype(jnp.float32)
    slots = slot_index.reshape(N_EXP, N_REP, TOK_DEV)
    onehot = (slots[:, :, :, None] == jnp.arange(CAP, dtype=jnp.int32)[None, None, None, :]).astype(jnp.float32)
    routed = jnp.einsum('erts,ertd->resd', onehot, blocks).astype(jnp.bfloat16)
    routed = routed.reshape(N_REP * N_EXP * CAP, D)
    preact = jnp.dot(routed, weights.reshape(D, 2 * FF), preferred_element_type=jnp.float32)
    preact = preact.reshape(N_REP * N_EXP * CAP, 2, FF)
    hidden = (jax.nn.silu(preact[:, 0]) * preact[:, 1]).astype(jnp.bfloat16)
    return (new_master, new_first, new_second, hidden.reshape(N_REP, N_EXP * CAP, FF))
```

```python
import functools

import jax
import jax.numpy as jnp
from jax import lax
from jax.experimental import pallas as pl
from jax.experimental.pallas import tpu as pltpu
from jax.sharding import PartitionSpec as P

STEP = 100


def largest_block(size, most):
    block = most
    while size % block:
        block //= 2
    return block


def adam_kernel(replicas, passed, rows_ref, cot_ref, pieces_ref, master_ref, first_ref, second_ref, *rest):
    out_master, out_first, out_second, out_pre = rest[passed:]
    width = master_ref.shape[2]
    correct_one = 1.0 - 0.9**STEP
    correct_two = 1.0 - 0.999**STEP

    @pl.when(pl.program_id(0) == 0)
    def _():
        out_pre[...] = jnp.zeros_like(out_pre)

    for g in range(2):
        cols = slice(g * width, (g + 1) * width)
        total = jnp.dot(rows_ref[...], cot_ref[:, cols], preferred_element_type=jnp.float32)
        average = total / replicas
        new_first = 0.9 * first_ref[:, g, :] + 0.1 * average
        new_second = 0.999 * second_ref[:, g, :] + 0.001 * average * average
        ratio = new_first / correct_one / (jnp.sqrt(new_second / correct_two) + 1e-08)
        old = master_ref[:, g, :]
        new_master = old - 0.001 * (ratio + 0.1 * old)
        out_first[:, g, :] = new_first
        out_second[:, g, :] = new_second
        out_master[:, g, :] = new_master
        out_pre[:, cols] += jnp.dot(
            pieces_ref[...], new_master.astype(jnp.bfloat16), preferred_element_type=jnp.float32
        )


def adam_chunk(chunk, width, replicas, rows_t, cot, pieces, master, first, second, before):
    share, depth = rows_t.shape
    routed_rows = pieces.shape[0]
    block = largest_block(share, 256)
    state = pl.BlockSpec((block, 2, width), lambda i: (i, 0, chunk))
    shape = jax.ShapeDtypeStruct(master.shape, jnp.float32)
    passed = len(before)
    return pl.pallas_call(
        functools.partial(adam_kernel, replicas, passed),
        grid=(share // block,),
        in_specs=[
            pl.BlockSpec((block, depth), lambda i: (i, 0)),
            pl.BlockSpec((depth, 2 * width), lambda i: (0, 0)),
            pl.BlockSpec((routed_rows, block), lambda i: (0, i)),
            state,
            state,
            state,
        ]
        + [pl.BlockSpec(memory_space=pl.ANY)] * passed,
        out_specs=[state, state, state, pl.BlockSpec((routed_rows, 2 * width), lambda i: (0, 0))],
        out_shape=[shape, shape, shape, jax.ShapeDtypeStruct((routed_rows, 2 * width), jnp.float32)],
        input_output_aliases={6 + i: i for i in range(passed)},
        cost_estimate=pl.CostEstimate(
            flops=2 * share * depth * 2 * width,
            bytes_accessed=24 * share * 2 * width + 2 * share * depth,
            transcendentals=0,
        ),
        compiler_params=pltpu.CompilerParams(vmem_limit_bytes=40 * 1024 * 1024),
    )(rows_t, cot, pieces, master, first, second, *before)


def shards(tokens, slot_index, saved_inputs, cotangents, master, moment1, moment2):
    replicas = lax.axis_size("rep")
    peers = lax.axis_size("exp")
    rows_in = saved_inputs[0]
    saved, feature_width = rows_in.shape
    hidden_dev = cotangents.shape[3]
    row_share = feature_width // replicas
    contract_rows = (((0,), (0,)), ((), ()))

    capacity = tokens.shape[0] // 4
    onehot = (slot_index[:, None] == jnp.arange(capacity, dtype=jnp.int32)[None, :]).astype(
        jnp.bfloat16
    )
    chosen = lax.dot_general(
        onehot, tokens, contract_rows, preferred_element_type=jnp.float32
    ).astype(jnp.bfloat16)
    routed = lax.all_gather(chosen, "exp", axis=0, tiled=True)
    pieces = lax.all_to_all(routed, "rep", split_axis=1, concat_axis=0, tiled=True)

    part = saved // peers
    own = lax.dynamic_slice_in_dim(rows_in, lax.axis_index("exp") * part, part, 0)
    own = lax.all_to_all(own, "rep", split_axis=1, concat_axis=0, tiled=True)
    everyone = lax.all_gather(own, "exp", axis=0, tiled=True)
    everyone = everyone.reshape(peers, replicas, part, row_share)
    rows_t = everyone.transpose(3, 1, 0, 2).reshape(row_share, replicas * saved)

    width = max(128, hidden_dev // 4)
    outs = ()
    partials = []
    for chunk in range(hidden_dev // width):
        piece = cotangents[0, :, :, chunk * width : (chunk + 1) * width].reshape(saved, 2 * width)
        cot = lax.all_gather(piece, "rep", axis=0, tiled=True)
        *outs, pre = adam_chunk(
            chunk, width, replicas, rows_t, cot, pieces, master, moment1, moment2, tuple(outs)
        )
        partials.append(pre)
    preact = lax.psum_scatter(
        jnp.concatenate(partials, axis=1), "rep", scatter_dimension=0, tiled=True
    )
    preact = preact.reshape(routed.shape[0], hidden_dev // width, 2, width)
    hidden = (jax.nn.silu(preact[:, :, 0]) * preact[:, :, 1]).astype(jnp.bfloat16)
    return (*outs, hidden.reshape(1, routed.shape[0], hidden_dev))


def solution(mesh):
    return jax.shard_map(
        shards,
        mesh=mesh,
        in_specs=(
            P(("exp", "rep"), None),
            P(("exp", "rep")),
            P("rep", None, None),
            P("rep", None, None, "exp"),
            P("rep", None, "exp"),
            P("rep", None, "exp"),
            P("rep", None, "exp"),
        ),
        out_specs=(
            P("rep", None, "exp"),
            P("rep", None, "exp"),
            P("rep", None, "exp"),
            P("rep", None, "exp"),
        ),
        check_vma=False,
    )
```

```python
import functools

import jax
import jax.numpy as jnp
from jax import lax
from jax.experimental import pallas as pl
from jax.experimental.pallas import tpu as pltpu
from jax.sharding import PartitionSpec as P

STEP = 100


def largest_block(size, most):
    block = most
    while size % block:
        block //= 2
    return block


def adam_kernel(replicas, passed, rows_ref, cot_ref, pieces_ref, master_ref, first_ref, second_ref, *rest):
    out_master, out_first, out_second, out_pre = rest[passed:]
    width = master_ref.shape[2]
    correct_one = 1.0 - 0.9**STEP
    correct_two = 1.0 - 0.999**STEP

    @pl.when(pl.program_id(0) == 0)
    def _():
        out_pre[...] = jnp.zeros_like(out_pre)

    for g in range(2):
        cols = slice(g * width, (g + 1) * width)
        total = jnp.dot(rows_ref[...], cot_ref[:, cols], preferred_element_type=jnp.float32)
        average = total / replicas
        new_first = 0.9 * first_ref[:, g, :] + 0.1 * average
        new_second = 0.999 * second_ref[:, g, :] + 0.001 * average * average
        ratio = new_first / correct_one / (jnp.sqrt(new_second / correct_two) + 1e-08)
        old = master_ref[:, g, :]
        new_master = old - 0.001 * (ratio + 0.1 * old)
        out_first[:, g, :] = new_first
        out_second[:, g, :] = new_second
        out_master[:, g, :] = new_master
        out_pre[:, cols] += jnp.dot(
            pieces_ref[...], new_master.astype(jnp.bfloat16), preferred_element_type=jnp.float32
        )


def adam_chunk(chunk, width, replicas, rows_t, cot, pieces, master, first, second, before):
    share, depth = rows_t.shape
    routed_rows = pieces.shape[0]
    block = largest_block(share, 256)
    state = pl.BlockSpec((block, 2, width), lambda i: (i, 0, chunk))
    shape = jax.ShapeDtypeStruct(master.shape, jnp.float32)
    passed = len(before)
    return pl.pallas_call(
        functools.partial(adam_kernel, replicas, passed),
        grid=(share // block,),
        in_specs=[
            pl.BlockSpec((block, depth), lambda i: (i, 0)),
            pl.BlockSpec((depth, 2 * width), lambda i: (0, 0)),
            pl.BlockSpec((routed_rows, block), lambda i: (0, i)),
            state,
            state,
            state,
        ]
        + [pl.BlockSpec(memory_space=pl.ANY)] * passed,
        out_specs=[state, state, state, pl.BlockSpec((routed_rows, 2 * width), lambda i: (0, 0))],
        out_shape=[shape, shape, shape, jax.ShapeDtypeStruct((routed_rows, 2 * width), jnp.float32)],
        input_output_aliases={6 + i: i for i in range(passed)},
        cost_estimate=pl.CostEstimate(
            flops=2 * share * depth * 2 * width,
            bytes_accessed=24 * share * 2 * width + 2 * share * depth,
            transcendentals=0,
        ),
        compiler_params=pltpu.CompilerParams(vmem_limit_bytes=40 * 1024 * 1024),
    )(rows_t, cot, pieces, master, first, second, *before)


def shards(tokens, slot_index, saved_inputs, cotangents, master, moment1, moment2):
    replicas = lax.axis_size("rep")
    peers = lax.axis_size("exp")
    rows_in = saved_inputs[0]
    saved, feature_width = rows_in.shape
    hidden_dev = cotangents.shape[3]
    row_share = feature_width // replicas
    contract_rows = (((0,), (0,)), ((), ()))

    capacity = tokens.shape[0] // 4
    onehot = (slot_index[:, None] == jnp.arange(capacity, dtype=jnp.int32)[None, :]).astype(
        jnp.bfloat16
    )
    chosen = lax.dot_general(
        onehot, tokens, contract_rows, preferred_element_type=jnp.float32
    ).astype(jnp.bfloat16)
    routed = lax.all_gather(chosen, "exp", axis=0, tiled=True)
    pieces = lax.all_to_all(routed, "rep", split_axis=1, concat_axis=0, tiled=True)

    width = max(128, hidden_dev // 4)
    chunks = hidden_dev // width
    sent = [
        cotangents[0, :, :, chunk * width : (chunk + 1) * width].reshape(saved, 2 * width)
        for chunk in range(chunks)
    ]
    part = saved // peers
    own = lax.dynamic_slice_in_dim(rows_in, lax.axis_index("exp") * part, part, 0)
    cots = [lax.all_gather(sent[0], "rep", axis=0, tiled=True)]
    own, sent[0] = lax.optimization_barrier((own, sent[0]))
    own = lax.all_to_all(own, "rep", split_axis=1, concat_axis=0, tiled=True)
    own, cots[0] = lax.optimization_barrier((own, cots[0]))
    everyone = lax.all_gather(own, "exp", axis=0, tiled=True)
    for chunk in range(1, chunks):
        sent[chunk], own = lax.optimization_barrier((sent[chunk], own))
        cots.append(lax.all_gather(sent[chunk], "rep", axis=0, tiled=True))
    everyone = everyone.reshape(peers, replicas, part, row_share)
    rows_t = everyone.transpose(3, 1, 0, 2).reshape(row_share, replicas * saved)

    outs = ()
    hidden = []
    own_rows = routed.shape[0]
    for chunk in range(chunks):
        *outs, pre = adam_chunk(
            chunk, width, replicas, rows_t, cots[chunk], pieces, master, moment1, moment2, tuple(outs)
        )
        terms = lax.all_to_all(
            pre.reshape(replicas, own_rows, 2 * width), "rep", split_axis=0, concat_axis=0, tiled=True
        )
        if chunk + 1 < chunks:
            terms, cots[chunk + 1] = lax.optimization_barrier((terms, cots[chunk + 1]))
        preact = jnp.sum(terms, axis=0)
        hidden.append((jax.nn.silu(preact[:, :width]) * preact[:, width:]).astype(jnp.bfloat16))
    return (*outs, jnp.concatenate(hidden, axis=1)[None])


def solution(mesh):
    return jax.shard_map(
        shards,
        mesh=mesh,
        in_specs=(
            P(("exp", "rep"), None),
            P(("exp", "rep")),
            P("rep", None, None),
            P("rep", None, None, "exp"),
            P("rep", None, "exp"),
            P("rep", None, "exp"),
            P("rep", None, "exp"),
        ),
        out_specs=(
            P("rep", None, "exp"),
            P("rep", None, "exp"),
            P("rep", None, "exp"),
            P("rep", None, "exp"),
        ),
        check_vma=False,
    )
```

```python
import functools

import jax
import jax.numpy as jnp
from jax import lax
from jax.experimental import pallas as pl
from jax.experimental.pallas import tpu as pltpu
from jax.sharding import PartitionSpec as P

STEP = 100


def largest_block(size, most):
    block = most
    while size % block:
        block //= 2
    return block


def adam_kernel(replicas, passed, rows_ref, cot_ref, pieces_ref, master_ref, first_ref, second_ref, *rest):
    out_master, out_first, out_second, out_pre = rest[passed:]
    width = master_ref.shape[2]
    correct_one = 1.0 - 0.9**STEP
    correct_two = 1.0 - 0.999**STEP

    @pl.when(pl.program_id(0) == 0)
    def _():
        out_pre[...] = jnp.zeros_like(out_pre)

    for g in range(2):
        cols = slice(g * width, (g + 1) * width)
        total = jnp.dot(rows_ref[...], cot_ref[:, cols], preferred_element_type=jnp.float32)
        average = total * (1.0 / replicas)
        new_first = 0.9 * first_ref[:, g, :] + 0.1 * average
        new_second = 0.999 * second_ref[:, g, :] + 0.001 * average * average
        ratio = new_first * (1.0 / correct_one) / (jnp.sqrt(new_second * (1.0 / correct_two)) + 1e-08)
        old = master_ref[:, g, :]
        new_master = old - 0.001 * (ratio + 0.1 * old)
        out_first[:, g, :] = new_first
        out_second[:, g, :] = new_second
        out_master[:, g, :] = new_master
        out_pre[:, cols] += jnp.dot(
            pieces_ref[...], new_master.astype(jnp.bfloat16), preferred_element_type=jnp.float32
        )


def adam_chunk(chunk, width, replicas, rows_t, cot, pieces, master, first, second, before):
    share, depth = rows_t.shape
    routed_rows = pieces.shape[0]
    block = largest_block(share, 256)
    state = pl.BlockSpec((block, 2, width), lambda i: (i, 0, chunk))
    shape = jax.ShapeDtypeStruct(master.shape, jnp.float32)
    passed = len(before)
    return pl.pallas_call(
        functools.partial(adam_kernel, replicas, passed),
        grid=(share // block,),
        in_specs=[
            pl.BlockSpec((block, depth), lambda i: (i, 0)),
            pl.BlockSpec((depth, 2 * width), lambda i: (0, 0)),
            pl.BlockSpec((routed_rows, block), lambda i: (0, i)),
            state,
            state,
            state,
        ]
        + [pl.BlockSpec(memory_space=pl.ANY)] * passed,
        out_specs=[state, state, state, pl.BlockSpec((routed_rows, 2 * width), lambda i: (0, 0))],
        out_shape=[shape, shape, shape, jax.ShapeDtypeStruct((routed_rows, 2 * width), jnp.float32)],
        input_output_aliases={6 + i: i for i in range(passed)},
        cost_estimate=pl.CostEstimate(
            flops=2 * share * depth * 2 * width,
            bytes_accessed=24 * share * 2 * width + 2 * share * depth,
            transcendentals=0,
        ),
        compiler_params=pltpu.CompilerParams(vmem_limit_bytes=56 * 1024 * 1024),
    )(rows_t, cot, pieces, master, first, second, *before)


def gather_rows(own, peers):
    replicas = lax.axis_size("rep")
    part, row_share = own.shape[0] // replicas, own.shape[1]
    bits = peers.bit_length() - 1
    if bits < 2 or peers != 1 << bits or row_share % 2:
        return lax.all_gather(own, "exp", axis=0).reshape(peers, replicas, part, row_share)
    me = lax.axis_index("exp")
    upper = list(range(1, bits))
    half = row_share // 2
    chains = [
        own[:, h * half : (h + 1) * half].reshape((1,) * bits + (replicas, part, half))
        for h in range(2)
    ]
    orders = [upper + [0], upper[::-1] + [0]]
    for step in range(bits):
        arrived = [
            lax.ppermute(chain, "exp", [(i, i ^ (1 << order[step])) for i in range(peers)])
            for chain, order in zip(chains, orders)
        ]
        for h in range(2):
            bit = orders[h][step]
            odd = (me >> bit) % 2 == 1
            low = jnp.where(odd, arrived[h], chains[h])
            high = jnp.where(odd, chains[h], arrived[h])
            chains[h] = jnp.concatenate([low, high], axis=bits - 1 - bit)
    return jnp.concatenate(
        [chain.reshape(peers, replicas, part, half) for chain in chains], axis=3
    )


def shards(tokens, slot_index, saved_inputs, cotangents, master, moment1, moment2):
    replicas = lax.axis_size("rep")
    peers = lax.axis_size("exp")
    rows_in = saved_inputs[0]
    saved, feature_width = rows_in.shape
    hidden_dev = cotangents.shape[3]
    row_share = feature_width // replicas
    contract_rows = (((0,), (0,)), ((), ()))

    capacity = tokens.shape[0] // 4
    onehot = (slot_index[:, None] == jnp.arange(capacity, dtype=jnp.int32)[None, :]).astype(
        jnp.bfloat16
    )
    chosen = lax.dot_general(
        onehot, tokens, contract_rows, preferred_element_type=jnp.float32
    ).astype(jnp.bfloat16)
    routed = lax.all_gather(chosen, "exp", axis=0, tiled=True)
    pieces = lax.all_to_all(routed, "rep", split_axis=1, concat_axis=0, tiled=True)

    if hidden_dev % 1024 == 0:
        unit = hidden_dev // 8
        spans = [(0, 2 * unit), (3 * unit, 3 * unit), (6 * unit, 2 * unit), (2 * unit, unit)]
    else:
        spans = [(0, hidden_dev)]
    chunks = len(spans)
    sent = [
        cotangents[0, :, :, start : start + width].reshape(saved, 2 * width)
        for start, width in spans
    ]
    part = saved // peers
    own = lax.dynamic_slice_in_dim(rows_in, lax.axis_index("exp") * part, part, 0)
    cots = [lax.all_gather(sent[0], "rep", axis=0, tiled=True)]
    own, sent[0] = lax.optimization_barrier((own, sent[0]))
    own = lax.all_to_all(own, "rep", split_axis=1, concat_axis=0, tiled=True)
    own, cots[0] = lax.optimization_barrier((own, cots[0]))
    everyone = gather_rows(own, peers)
    for chunk in range(1, chunks):
        sent[chunk], own = lax.optimization_barrier((sent[chunk], own))
        cots.append(lax.all_gather(sent[chunk], "rep", axis=0, tiled=True))
    rows_t = everyone.transpose(3, 1, 0, 2).reshape(row_share, replicas * saved)

    outs = ()
    hidden = []
    own_rows = routed.shape[0]
    for chunk in range(chunks):
        start, width = spans[chunk]
        *outs, pre = adam_chunk(
            start // width, width, replicas, rows_t, cots[chunk], pieces, master, moment1, moment2, tuple(outs)
        )
        terms = lax.all_to_all(
            pre.reshape(replicas, own_rows, 2 * width), "rep", split_axis=0, concat_axis=0, tiled=True
        )
        if chunk + 1 < chunks:
            terms, cots[chunk + 1] = lax.optimization_barrier((terms, cots[chunk + 1]))
        preact = jnp.sum(terms, axis=0)
        hidden.append((jax.nn.silu(preact[:, :width]) * preact[:, width:]).astype(jnp.bfloat16))
    hidden = [block for _, block in sorted(zip([start for start, _ in spans], hidden), key=lambda pair: pair[0])]
    return (*outs, jnp.concatenate(hidden, axis=1)[None])


def solution(mesh):
    return jax.shard_map(
        shards,
        mesh=mesh,
        in_specs=(
            P(("exp", "rep"), None),
            P(("exp", "rep")),
            P("rep", None, None),
            P("rep", None, None, "exp"),
            P("rep", None, "exp"),
            P("rep", None, "exp"),
            P("rep", None, "exp"),
        ),
        out_specs=(
            P("rep", None, "exp"),
            P("rep", None, "exp"),
            P("rep", None, "exp"),
            P("rep", None, "exp"),
        ),
        check_vma=False,
    )
```
